32 devices in a mesh: groups: 2 (over x), wide: 16 (over z, y, core).
Axes of the slice: x: 2, y: 2, z: 4, core: 2. Of those that a mesh axis runs over, the one named last changes fastest.
Arguments:
- picture_feature_maps: bfloat16 [256, 10, 10, 1536], P(('groups', 'wide')), parts along dimension 0, may hold values from -6 to 6
- partitioned_filter_tensor: bfloat16 [3, 3, 128, 1536], replicated, may hold values from -0.1875 to 0.1875
- picture_token_layer_scaling: float32 [1536], replicated, may hold values from 0.1 to 1.9
- summary_probes: bfloat16 [64, 1536], replicated, may hold values from -6 to 6
- summary_probe_layer_scaling: float32 [1536], replicated, may hold values from 0.1 to 1.9
- asking_projection_tensor: bfloat16 [1536, 1536], P('wide'), may hold values from -0.15625 to 0.15625
- lookup_projection_tensor: bfloat16 [1536, 1536], P('wide'), may hold values from -0.15625 to 0.15625
- content_projection_tensor: bfloat16 [1536, 1536], P('wide'), may hold values from -0.15625 to 0.15625
- final_projection_tensor: bfloat16 [1536, 1536], P(None, 'wide'), may hold values from -0.15625 to 0.15625
- sharpness_coefficient: float32 [16], replicated, may hold values from 0.5 to 64
Outputs:
- attended: float32 [128, 1536], P('groups'), parts along dimension 0
- new_latents: bfloat16 [128, 1536], P('groups'), parts along dimension 0
The draws below stay inside these ranges and needn't reach their ends.
There are 2 independent parts, one for each index of `groups`. The reference program is written for one: setup_inputs(seed, part) draws one part's arguments, and reference() takes and returns one part's arrays. A program takes and returns all parts, laid end to end along the dimension named above; an argument that names none is the same for every part. Nothing has to cross between parts.
All inputs are finite; a program needn't handle non-finite values.
Results may differ from the reference program's by a relative error of at most 0.004.
The reference program's roundings to bfloat16 on the way (of `activated`, `tok_norm`, `lat_norm` and `attention`) count: a program that leaves them out, or rounds other values in their place, can miss the bound.
Values may be sent and summed in bfloat16 or wider, within the bound.
A program may use at most 128 MiB of HBM per device.

```python
import jax
import jax.numpy as jnp
from jax import lax

D = 1536
GW = 128
FOCUS_CHANNELS = 16
SUMMARY_PROBES = 64
MAP = 10
F_DEV = 8
SUBSPACE_DIM = 96
FRAMES = 128
N_WIDE = 16


def draw_sharpness_coefficient(key, part):
    key_level, key_pick = jax.random.split(jax.random.fold_in(key, 17))
    levels = jax.random.uniform(key_level, (FOCUS_CHANNELS,), jnp.float32)
    chosen = jax.random.randint(key_pick, (), 0, FOCUS_CHANNELS)
    values = 0.5 * jnp.power(5.0, levels)
    highest = 2.5
    return jnp.where(jnp.arange(FOCUS_CHANNELS) == chosen, jnp.float32(highest), values).astype(jnp.float32)


def steps_of(key, shape, shards, least, high):
    def one(axis_at, shards_of):
        draws = jax.random.uniform(jax.random.fold_in(jax.random.fold_in(key, 6), axis_at), (shards_of,), jnp.float32, least / len(shards), high / len(shards))
        return jnp.repeat(jnp.exp(draws), shape[axis_at] // shards_of).reshape((-1,) + (1,) * (len(shape) - axis_at - 1))

    loudness = one(*shards[0])
    for cut in shards[1:]:
        loudness = loudness * one(*cut)
    return loudness


def bell_draw(key, extent, deviation, bound, cuts=(), dtype=jnp.bfloat16):
    result = jax.random.normal(key, extent, jnp.float32) * deviation
    if len(cuts) > 0:
        result = steps_of(key, extent, cuts, -0.22, 0.18) * result
    return jnp.clip(result, min=-bound, max=bound).astype(dtype)


def setup_inputs(seed: int = 0, part: int = 0) -> dict:
    streams_of = jax.random.split(jax.random.key(seed), 11)
    part_splits = jax.random.split(jax.random.fold_in(streams_of[10], part), 11)
    picture_feature_maps = bell_draw(part_splits[0], (FRAMES, MAP, MAP, D), 1.0, 6.0, ((0, 16),))
    partitioned_filter_tensor = bell_draw(streams_of[1], (3, 3, GW, D), (9 * GW) ** -0.5, 0.1875)
    picture_token_layer_scaling = jnp.clip(1.0 + 0.18 * jax.random.normal(streams_of[2], (D,), jnp.float32), 0.1, 1.9)
    summary_probes = bell_draw(streams_of[3], (SUMMARY_PROBES, D), 1.0, 6.0)
    summary_probe_layer_scaling = jnp.clip(1.0 + 0.18 * jax.random.normal(streams_of[4], (D,), jnp.float32), 0.1, 1.9)
    asking_projection_tensor = bell_draw(streams_of[5], (D, D), D ** -0.5, 0.15625, ((0, 16),))
    lookup_projection_tensor = bell_draw(streams_of[6], (D, D), D ** -0.5, 0.15625, ((0, 16),))
    content_projection_tensor = bell_draw(streams_of[7], (D, D), D ** -0.5, 0.15625, ((0, 16),))
    final_projection_tensor = bell_draw(streams_of[8], (D, D), D ** -0.5, 0.15625, ((1, 16),))
    sharpness_coefficient = draw_sharpness_coefficient(jax.random.fold_in(streams_of[10], 71), part)
    return dict(picture_feature_maps=picture_feature_maps, partitioned_filter_tensor=partitioned_filter_tensor, picture_token_layer_scaling=picture_token_layer_scaling, summary_probes=summary_probes, summary_probe_layer_scaling=summary_probe_layer_scaling, asking_projection_tensor=asking_projection_tensor, lookup_projection_tensor=lookup_projection_tensor, content_projection_tensor=content_projection_tensor, final_projection_tensor=final_projection_tensor, sharpness_coefficient=sharpness_coefficient)


RESIDUAL_SCALE = 0.2
EPSILON = 1e-06

def layer_norm(values, gain):
    center = values - lax.optimization_barrier(jnp.mean(values, axis=-1, keepdims=True))
    spread = lax.optimization_barrier(jnp.mean(center * center, axis=-1, keepdims=True))
    return center * lax.rsqrt(spread + EPSILON) * gain

def frame_block(block, partitioned_filter_tensor, picture_token_layer_scaling):
    activated = jax.nn.gelu(block.astype(jnp.float32)).astype(jnp.bfloat16)
    convolved = lax.conv_general_dilated(activated.astype(jnp.float32), partitioned_filter_tensor.astype(jnp.float32), (1, 1), 'SAME', dimension_numbers=('NHWC', 'HWIO', 'NHWC'), feature_group_count=D // GW, precision=lax.Precision.HIGHEST)
    summed = block.astype(jnp.float32) + RESIDUAL_SCALE * convolved
    return layer_norm(summed.reshape(-1, D), picture_token_layer_scaling).astype(jnp.bfloat16)

def reference(picture_feature_maps, partitioned_filter_tensor, picture_token_layer_scaling, summary_probes, summary_probe_layer_scaling, asking_projection_tensor, lookup_projection_tensor, content_projection_tensor, final_projection_tensor, sharpness_coefficient):
    blocks = picture_feature_maps.reshape(N_WIDE, F_DEV, MAP, MAP, D)
    tok_norm = lax.map(lambda block: frame_block(block, partitioned_filter_tensor, picture_token_layer_scaling), blocks).reshape(-1, D)
    lat_norm = layer_norm(summary_probes.astype(jnp.float32), summary_probe_layer_scaling).astype(jnp.bfloat16)
    probe_asking_vectors = jnp.dot(lat_norm, asking_projection_tensor, preferred_element_type=jnp.float32)
    rescaled_similarity_logits = probe_asking_vectors.reshape(SUMMARY_PROBES, FOCUS_CHANNELS, SUBSPACE_DIM) * (sharpness_coefficient / jnp.sqrt(jnp.float32(SUBSPACE_DIM)))[None, :, None]
    source = jnp.concatenate([tok_norm, lat_norm], axis=0)
    key_proj = jnp.dot(source, lookup_projection_tensor, preferred_element_type=jnp.float32).reshape(-1, FOCUS_CHANNELS, SUBSPACE_DIM)
    value_proj = jnp.dot(source, content_projection_tensor, preferred_element_type=jnp.float32).reshape(-1, FOCUS_CHANNELS, SUBSPACE_DIM)
    scores = jnp.einsum('lhd,thd->hlt', rescaled_similarity_logits, key_proj, precision=lax.Precision.HIGHEST)
    row_max = lax.optimization_barrier(jnp.max(scores, axis=-1, keepdims=True))
    weights = jnp.exp(scores - row_max)
    row_sum = lax.optimization_barrier(jnp.sum(weights, axis=-1, keepdims=True))
    weighted = jnp.einsum('hlt,thd->hld', weights, value_proj, precision=lax.Precision.HIGHEST)
    attention = (weighted / row_sum).transpose(1, 0, 2).reshape(SUMMARY_PROBES, D).astype(jnp.bfloat16)
    attended = jnp.dot(attention, final_projection_tensor, preferred_element_type=jnp.float32)
    new_latents = (summary_probes.astype(jnp.float32) + attended).astype(jnp.bfloat16)
    return (attended, new_latents)
```

```python
import functools
import math

import jax
import jax.numpy as jnp
from jax import lax
from jax.experimental import pallas as pl
from jax.experimental.pallas import tpu as pltpu
from jax.sharding import PartitionSpec as P

RESIDUAL_SCALE = 0.2
EPSILON = 1e-06
LANES = 128
NT = (((1,), (1,)), ((), ()))


def layer_norm(values, gain):
    center = values - jnp.mean(values, axis=-1, keepdims=True)
    spread = jnp.mean(center * center, axis=-1, keepdims=True)
    return center * lax.rsqrt(spread + EPSILON) * gain


def window(head, breadth):
    start = head * breadth // LANES * LANES
    stop = -(-(head + 1) * breadth // LANES) * LANES
    return start, stop - start


def head_mask(head, breadth, shape):
    start, width = window(head, breadth)
    lane = lax.broadcasted_iota(jnp.int32, shape, len(shape) - 1) + start
    return (lane >= head * breadth) & (lane < (head + 1) * breadth)


def halves(values):
    high = values.astype(jnp.bfloat16)
    low = (values - high.astype(jnp.float32)).astype(jnp.bfloat16)
    return high, low


def mixer(
    n, heads, tok_count,
    tok_ref, lat_own_ref, lat_slice_ref, probes_ref, sharp_ref,
    wq_ref, wk_ref, wv_ref, wo_ref,
    attended_ref, new_ref,
    gathered, qpart, qrecv, qall, queries, source, u_high, u_low,
    wsum, part, received, att_all, att_low, cols_all,
    z_send, y_send, core_send, w_recv, swap_send, swap_recv,
):
    channels = sharp_ref.shape[1]
    breadth = channels // heads
    lats = probes_ref.shape[0]
    rows = lats // n
    shard = wk_ref.shape[0]
    line = n // 4
    me = lax.axis_index("wide")
    core = lax.rem(me, 2)
    side = lax.rem(me // 2, 2)
    at = me // 4
    weights = (wk_ref, wv_ref)

    def place(a, b, c):
        return a * 4 + b * 2 + c

    def remote(src, dst, send, recv, target):
        return pltpu.make_async_remote_copy(
            src_ref=src, dst_ref=dst, send_sem=send, recv_sem=recv,
            device_id={"wide": target}, device_id_type=pl.DeviceIdType.MESH,
        )

    def ring(k):
        return lax.rem(me + k, n)

    def back(k):
        return lax.rem(me + n - k, n)

    def loop(count, body):
        def step(k, carry):
            body(k)
            return carry
        lax.fori_loop(1, count, step, 0)

    def swap(slot, src_of, dst, target, owner):
        return remote(
            src_of(target), dst.at[owner], swap_send.at[slot, target], swap_recv.at[slot, owner], target
        )

    def swap_start(slot, src_of, dst):
        loop(n, lambda k: swap(slot, src_of, dst, ring(k), me).start())

    def swap_wait(slot, src_of, dst):
        loop(n, lambda k: swap(slot, src_of, dst, ring(k), me).wait_send())
        loop(n, lambda k: swap(slot, src_of, dst, me, back(k)).wait_recv())

    def along(w, k):
        return remote(
            weights[w], gathered.at[w, me], z_send.at[w, k], w_recv.at[w, me],
            place(lax.rem(at + k, line), side, core),
        )

    def across(w, a):
        owner = place(a, side, core)
        return remote(
            gathered.at[w, owner], gathered.at[w, owner], y_send.at[w, a], w_recv.at[w, owner],
            place(at, 1 - side, core),
        )

    def over(w, a, b):
        owner = place(a, b, core)
        return remote(
            gathered.at[w, owner], gathered.at[w, owner], core_send.at[w, a * 2 + b],
            w_recv.at[w, owner], place(at, side, 1 - core),
        )

    def arrival(w, owner):
        remote(
            gathered.at[w, owner], gathered.at[w, owner], z_send.at[w, 0], w_recv.at[w, owner],
            place(at, side, 1 - core),
        ).wait_recv()

    def line_step(w, k):
        a = lax.rem(at + line - k, line)
        arrival(w, place(a, side, core))
        across(w, a).start()
        over(w, a, side).start()

    def far_step(w, k):
        a = lax.rem(at + line - k, line)
        arrival(w, place(a, 1 - side, core))
        over(w, a, 1 - side).start()

    def core_step(w, k):
        arrival(w, place(k // 2, lax.rem(k, 2), 1 - core))

    def finish_sends(w):
        def one(k, carry):
            across(w, k).wait_send()
            over(w, k, 0).wait_send()
            over(w, k, 1).wait_send()
            return carry
        loop(line, lambda k: along(w, k).wait_send())
        lax.fori_loop(0, line, one, 0)

    def each(count, body):
        def step(k, carry):
            body(k)
            return carry
        lax.fori_loop(0, count, step, 0)

    barrier = pltpu.get_barrier_semaphore()
    loop(n, lambda k: pl.semaphore_signal(
        barrier, inc=1, device_id={"wide": ring(k)}, device_id_type=pl.DeviceIdType.MESH))
    pl.semaphore_wait(barrier, n - 1)

    partial = jnp.dot(lat_slice_ref[...], wq_ref[...], preferred_element_type=jnp.float32)
    for j in range(n):
        qpart[j] = partial[j * rows:(j + 1) * rows]
    qrecv[me] = qpart[me]
    swap_start(0, lambda j: qpart.at[j], qrecv)
    for w in range(2):
        gathered[w, me] = weights[w][...]
        loop(line, lambda k: along(w, k).start())
        across(w, at).start()
        over(w, at, side).start()

    source[:tok_count] = tok_ref[...]
    source[tok_count:] = lat_own_ref[...]

    swap_wait(0, lambda j: qpart.at[j], qrecv)
    qall[me] = jnp.sum(qrecv[...], axis=0) * sharp_ref[...]
    swap_start(1, lambda j: qall.at[me], qall)

    loop(line, lambda k: line_step(0, k))
    each(line, lambda k: far_step(0, k))
    loop(line, lambda k: line_step(1, k))
    swap_wait(1, lambda j: qall.at[me], qall)
    for j in range(n):
        queries[j * rows:(j + 1) * rows] = qall[j]
    each(n // 2, lambda k: core_step(0, k))

    total = source.shape[0]
    per_block = max(1, min(heads, 256 // lats))
    lane = lax.broadcasted_iota(jnp.int32, (lats, LANES), 1)
    stat_max = jnp.zeros((lats, LANES), jnp.float32)
    stat_sum = jnp.zeros((lats, LANES), jnp.float32)
    for first in range(0, heads, per_block):
        folded = []
        for head in range(first, first + per_block):
            start, width = window(head, breadth)
            part_q = queries[:, start:start + width]
            part_q = jnp.where(head_mask(head, breadth, part_q.shape), part_q, 0.0)
            both = jnp.concatenate(halves(part_q), axis=0)
            look = gathered[0, :, :, start:start + width].astype(jnp.bfloat16)
            look = look.reshape(n * shard, width)
            raw = lax.dot_general(both, look, NT, preferred_element_type=jnp.float32)
            folded.append(raw[:lats] + raw[lats:])
        high, low = halves(jnp.concatenate(folded, axis=0))
        scores = lax.dot_general(high, source[...], NT, preferred_element_type=jnp.float32)
        scores += lax.dot_general(low, source[...], NT, preferred_element_type=jnp.float32)
        column = lax.broadcasted_iota(jnp.int32, scores.shape, 1)
        scores = jnp.where(column < tok_count + rows, scores, -jnp.inf)
        row_max = jnp.max(scores, axis=1, keepdims=True)
        terms = jnp.exp(scores - row_max).astype(jnp.bfloat16)
        row_sum = jnp.sum(terms.astype(jnp.float32), axis=1, keepdims=True)
        mixed = jnp.dot(terms, source[...], preferred_element_type=jnp.float32)
        high, low = halves(mixed)
        u_high[first * lats:(first + per_block) * lats] = high
        u_low[first * lats:(first + per_block) * lats] = low
        for i in range(per_block):
            stat_max = jnp.where(lane == first + i, row_max[i * lats:(i + 1) * lats], stat_max)
            stat_sum = jnp.where(lane == first + i, row_sum[i * lats:(i + 1) * lats], stat_sum)
        if first == 0:
            each(line, lambda k: far_step(1, k))
    each(n // 2, lambda k: core_step(1, k))

    wsum[...] = jnp.zeros_like(wsum)
    for head in range(heads):
        start, width = window(head, breadth)
        both = jnp.concatenate(
            [u_high[head * lats:(head + 1) * lats], u_low[head * lats:(head + 1) * lats]], axis=0
        )
        content = gathered[1, :, :, start:start + width].astype(jnp.bfloat16)
        raw = jnp.dot(both, content.reshape(n * shard, width), preferred_element_type=jnp.float32)
        raw = raw[:lats] + raw[lats:]
        wsum[:, start:start + width] += jnp.where(head_mask(head, breadth, raw.shape), raw, 0.0)
    for j in range(n):
        cut = slice(j * rows, (j + 1) * rows)
        part[j, :, :channels] = wsum[cut]
        part[j, :, channels:channels + LANES] = stat_max[cut]
        part[j, :, channels + LANES:] = stat_sum[cut]
    received[me] = part[me]
    swap_start(2, lambda j: part.at[j], received)
    swap_wait(2, lambda j: part.at[j], received)

    maxima = received[:, :, channels:channels + LANES]
    factor = jnp.exp(maxima - jnp.max(maxima, axis=0, keepdims=True))
    joint = jnp.sum(received[:, :, channels + LANES:] * factor, axis=0, keepdims=True)
    factor = factor / jnp.where(joint > 0.0, joint, 1.0)
    att_all[me] = jnp.zeros((rows, channels), jnp.float32)
    for head in range(heads):
        start, width = window(head, breadth)
        scaled = received[:, :, start:start + width] * factor[:, :, head:head + 1]
        scaled = jnp.sum(scaled, axis=0)
        keep = head_mask(head, breadth, scaled.shape)
        att_all[me, :, start:start + width] += jnp.where(keep, scaled, 0.0)
    swap_start(3, lambda j: att_all.at[me], att_all)
    swap_wait(3, lambda j: att_all.at[me], att_all)
    for j in range(n):
        wsum[j * rows:(j + 1) * rows] = att_all[j]
    att_low[...] = wsum[...].astype(jnp.bfloat16)
    cols_all[me] = jnp.dot(att_low[...], wo_ref[...], preferred_element_type=jnp.float32)
    swap_start(4, lambda j: cols_all.at[me], cols_all)
    swap_wait(4, lambda j: cols_all.at[me], cols_all)
    wide = wo_ref.shape[1]
    for j in range(n):
        attended_ref[:, j * wide:(j + 1) * wide] = cols_all[j]
    new_ref[...] = (probes_ref[...].astype(jnp.float32) + attended_ref[...]).astype(jnp.bfloat16)
    finish_sends(0)
    finish_sends(1)


def per_device(
    n,
    picture_feature_maps,
    partitioned_filter_tensor,
    picture_token_layer_scaling,
    summary_probes,
    summary_probe_layer_scaling,
    asking_projection_tensor,
    lookup_projection_tensor,
    content_projection_tensor,
    final_projection_tensor,
    sharpness_coefficient,
):
    channels = picture_feature_maps.shape[3]
    heads = sharpness_coefficient.shape[0]
    breadth = channels // heads
    lats = summary_probes.shape[0]
    activated = jax.nn.gelu(picture_feature_maps.astype(jnp.float32)).astype(jnp.bfloat16)
    convolved = lax.conv_general_dilated(
        activated,
        partitioned_filter_tensor,
        (1, 1),
        "SAME",
        dimension_numbers=("NHWC", "HWIO", "NHWC"),
        feature_group_count=channels // partitioned_filter_tensor.shape[2],
        preferred_element_type=jnp.float32,
    )
    summed = picture_feature_maps.astype(jnp.float32) + RESIDUAL_SCALE * convolved
    tok_norm = layer_norm(summed.reshape(-1, channels), picture_token_layer_scaling).astype(
        jnp.bfloat16
    )
    lat_norm = layer_norm(summary_probes.astype(jnp.float32), summary_probe_layer_scaling).astype(
        jnp.bfloat16
    )
    tok_count = tok_norm.shape[0]
    shard = asking_projection_tensor.shape[0]
    rows = lats // n
    me = lax.axis_index("wide")
    lat_slice = lax.dynamic_slice_in_dim(lat_norm, me * shard, shard, 1)
    lat_own = lax.dynamic_slice_in_dim(lat_norm, me * rows, rows, 0)
    extra = -(-rows // 16) * 16
    lat_own = jnp.pad(lat_own, ((0, extra - rows), (0, 0)))
    sharp = jnp.repeat(sharpness_coefficient / math.sqrt(breadth), breadth)[None, :]
    lookup, content = lookup_projection_tensor, content_projection_tensor
    wire = jnp.bfloat16 if shard % 16 == 0 else jnp.float32
    lookup, content = lookup.astype(wire), content.astype(wire)
    vmem = pl.BlockSpec(memory_space=pltpu.VMEM)
    f32, bf16 = jnp.float32, jnp.bfloat16
    width = final_projection_tensor.shape[1]
    line = n // 4
    return pl.pallas_call(
        functools.partial(mixer, n, heads, tok_count),
        out_shape=(
            jax.ShapeDtypeStruct((lats, channels), f32),
            jax.ShapeDtypeStruct((lats, channels), bf16),
        ),
        in_specs=[vmem] * 9,
        out_specs=(vmem, vmem),
        scratch_shapes=[
            pltpu.VMEM((2, n, shard, channels), wire),
            pltpu.VMEM((n, rows, channels), f32),
            pltpu.VMEM((n, rows, channels), f32),
            pltpu.VMEM((n, rows, channels), f32),
            pltpu.VMEM((lats, channels), f32),
            pltpu.VMEM((tok_count + extra, channels), bf16),
            pltpu.VMEM((heads * lats, channels), bf16),
            pltpu.VMEM((heads * lats, channels), bf16),
            pltpu.VMEM((lats, channels), f32),
            pltpu.VMEM((n, rows, channels + 2 * LANES), f32),
            pltpu.VMEM((n, rows, channels + 2 * LANES), f32),
            pltpu.VMEM((n, rows, channels), f32),
            pltpu.VMEM((lats, channels), bf16),
            pltpu.VMEM((n, lats, width), f32),
            pltpu.SemaphoreType.DMA((2, line)),
            pltpu.SemaphoreType.DMA((2, line)),
            pltpu.SemaphoreType.DMA((2, 2 * line)),
            pltpu.SemaphoreType.DMA((2, n)),
            pltpu.SemaphoreType.DMA((5, n)),
            pltpu.SemaphoreType.DMA((5, n)),
        ],
        compiler_params=pltpu.CompilerParams(
            collective_id=0, has_side_effects=True, vmem_limit_bytes=56 * 1024 * 1024
        ),
    )(
        tok_norm, lat_own, lat_slice, summary_probes, sharp,
        asking_projection_tensor, lookup, content, final_projection_tensor,
    )


def solution(mesh):
    placed = (
        P(("groups", "wide"), None, None, None),
        P(),
        P(),
        P(),
        P(),
        P("wide", None),
        P("wide", None),
        P("wide", None),
        P(None, "wide"),
        P(),
    )
    return jax.shard_map(
        functools.partial(per_device, mesh.shape["wide"]),
        mesh=mesh,
        in_specs=placed,
        out_specs=(P("groups", None), P("groups", None)),
        check_vma=False,
    )
```

```python
import functools
import math

import jax
import jax.numpy as jnp
import numpy as np
from jax import lax
from jax.experimental import pallas as pl
from jax.experimental.pallas import tpu as pltpu
from jax.sharding import PartitionSpec as P

RESIDUAL_SCALE = 0.2
EPSILON = 1e-06
LANES = 128
NT = (((1,), (1,)), ((), ()))


def layer_norm(values, gain):
    center = values - jnp.mean(values, axis=-1, keepdims=True)
    spread = jnp.mean(center * center, axis=-1, keepdims=True)
    return center * lax.rsqrt(spread + EPSILON) * gain


def window(head, breadth):
    start = head * breadth // LANES * LANES
    stop = -(-(head + 1) * breadth // LANES) * LANES
    return start, stop - start


def head_mask(head, breadth, shape):
    start, width = window(head, breadth)
    lane = lax.broadcasted_iota(jnp.int32, shape, len(shape) - 1) + start
    return (lane >= head * breadth) & (lane < (head + 1) * breadth)


def halves(values):
    high = values.astype(jnp.bfloat16)
    low = (values - high.astype(jnp.float32)).astype(jnp.bfloat16)
    return high, low


def mixer(
    n, heads,
    maps_ref, filter_ref, gain_ref, pick_ref, lat_own_ref, lat_slice_ref, probes_ref, sharp_ref,
    wq_ref, wk_ref, wv_ref, wo_ref,
    attended_ref, new_ref,
    gathered, qpart, qrecv, qall, queries, source, u_high, u_low,
    wsum, part, received, att_all, att_low, cols_all,
    plain, act, summed,
    z_send, y_send, core_send, w_recv, swap_send, swap_recv,
):
    channels = sharp_ref.shape[1]
    breadth = channels // heads
    lats = probes_ref.shape[0]
    rows = lats // n
    shard = wk_ref.shape[0]
    line = n // 4
    me = lax.axis_index("wide")
    core = lax.rem(me, 2)
    side = lax.rem(me // 2, 2)
    at = me // 4
    weights = (wk_ref, wv_ref)

    def place(a, b, c):
        return a * 4 + b * 2 + c

    def remote(src, dst, send, recv, target):
        return pltpu.make_async_remote_copy(
            src_ref=src, dst_ref=dst, send_sem=send, recv_sem=recv,
            device_id={"wide": target}, device_id_type=pl.DeviceIdType.MESH,
        )

    def ring(k):
        return lax.rem(me + k, n)

    def back(k):
        return lax.rem(me + n - k, n)

    def loop(count, body):
        def step(k, carry):
            body(k)
            return carry
        lax.fori_loop(1, count, step, 0)

    def swap(slot, src_of, dst, target, owner):
        return remote(
            src_of(target), dst.at[owner], swap_send.at[slot, target], swap_recv.at[slot, owner], target
        )

    def swap_start(slot, src_of, dst):
        loop(n, lambda k: swap(slot, src_of, dst, ring(k), me).start())

    def swap_wait(slot, src_of, dst):
        loop(n, lambda k: swap(slot, src_of, dst, ring(k), me).wait_send())
        loop(n, lambda k: swap(slot, src_of, dst, me, back(k)).wait_recv())

    def along(w, k):
        return remote(
            weights[w], gathered.at[w, me], z_send.at[w, k], w_recv.at[w, me],
            place(lax.rem(at + k, line), side, core),
        )

    def across(w, a):
        owner = place(a, side, core)
        return remote(
            gathered.at[w, owner], gathered.at[w, owner], y_send.at[w, a], w_recv.at[w, owner],
            place(at, 1 - side, core),
        )

    def over(w, a, b):
        owner = place(a, b, core)
        return remote(
            gathered.at[w, owner], gathered.at[w, owner], core_send.at[w, a * 2 + b],
            w_recv.at[w, owner], place(at, side, 1 - core),
        )

    def arrival(w, owner):
        remote(
            gathered.at[w, owner], gathered.at[w, owner], z_send.at[w, 0], w_recv.at[w, owner],
            place(at, side, 1 - core),
        ).wait_recv()

    def line_step(w, k):
        a = lax.rem(at + line - k, line)
        arrival(w, place(a, side, core))
        across(w, a).start()
        over(w, a, side).start()

    def far_step(w, k):
        a = lax.rem(at + line - k, line)
        arrival(w, place(a, 1 - side, core))
        over(w, a, 1 - side).start()

    def core_step(w, k):
        arrival(w, place(k // 2, lax.rem(k, 2), 1 - core))

    def finish_sends(w):
        def one(k, carry):
            across(w, k).wait_send()
            over(w, k, 0).wait_send()
            over(w, k, 1).wait_send()
            return carry
        loop(line, lambda k: along(w, k).wait_send())
        lax.fori_loop(0, line, one, 0)

    def each(count, body):
        def step(k, carry):
            body(k)
            return carry
        lax.fori_loop(0, count, step, 0)

    barrier = pltpu.get_barrier_semaphore()
    loop(n, lambda k: pl.semaphore_signal(
        barrier, inc=1, device_id={"wide": ring(k)}, device_id_type=pl.DeviceIdType.MESH))
    pl.semaphore_wait(barrier, n - 1)

    partial = jnp.dot(lat_slice_ref[...], wq_ref[...], preferred_element_type=jnp.float32)
    for j in range(n):
        qpart[j] = partial[j * rows:(j + 1) * rows]
    qrecv[me] = qpart[me]
    swap_start(0, lambda j: qpart.at[j], qrecv)

    def send_own(w):
        gathered[w, me] = weights[w][...]
        loop(line, lambda k: along(w, k).start())
        across(w, at).start()
        over(w, at, side).start()

    send_own(0)
    frames, high_side, wide_side = maps_ref.shape[:3]
    group = filter_ref.shape[0] // 9
    at_once = plain.shape[0]
    pitch = plain.shape[2]
    flat = high_side * pitch
    steps = frames // at_once
    packed = pick_ref.shape[0]
    real = at_once * high_side * wide_side
    tok_count = steps * packed
    plain[...] = jnp.zeros_like(plain)
    act[...] = jnp.zeros_like(act)
    source[tok_count:] = lat_own_ref[...]

    def convolve(i):
        for f in range(at_once):
            plain[f, :, :wide_side] = maps_ref[i * at_once + f].astype(jnp.float32)
            g = jax.nn.gelu(plain[f]).reshape(flat, channels)
            act[f, 0, pitch:pitch + flat] = pltpu.roll(g, 1, 0).astype(jnp.bfloat16)
            act[f, 1, pitch:pitch + flat] = g.astype(jnp.bfloat16)
            act[f, 2, pitch:pitch + flat] = pltpu.roll(g, flat - 1, 0).astype(jnp.bfloat16)
        for c in range(channels // group):
            cut = slice(c * group, (c + 1) * group)
            taps = jnp.concatenate([
                jnp.concatenate([
                    act[f, dx, dy * pitch:dy * pitch + flat, cut]
                    for dy in range(3) for dx in range(3)
                ], axis=1)
                for f in range(at_once)
            ], axis=0)
            summed[:, cut] = jnp.dot(
                taps, filter_ref[:, cut], preferred_element_type=jnp.float32)
        normed = []
        for f in range(at_once):
            rows_of = slice(f * flat, (f + 1) * flat)
            value = plain[f].reshape(flat, channels) + RESIDUAL_SCALE * summed[rows_of]
            normed.append(layer_norm(value, gain_ref[...]).astype(jnp.bfloat16))
        dense = jnp.dot(
            pick_ref[...], jnp.concatenate(normed, axis=0), preferred_element_type=jnp.float32)
        where = pl.multiple_of(i * packed, 16)
        source[pl.ds(where, packed)] = dense.astype(jnp.bfloat16)

    def conv_and_pass(i, carry):
        convolve(i)

        @pl.when((i >= 1) & (i < line))
        def _():
            line_step(0, i)
        return carry

    lax.fori_loop(0, steps, conv_and_pass, 0)

    def pass_on(k, carry):
        line_step(0, k)
        return carry

    lax.fori_loop(min(steps, line), line, pass_on, 0)
    send_own(1)

    swap_wait(0, lambda j: qpart.at[j], qrecv)
    qall[me] = jnp.sum(qrecv[...], axis=0) * sharp_ref[...]
    swap_start(1, lambda j: qall.at[me], qall)

    each(line, lambda k: far_step(0, k))
    swap_wait(1, lambda j: qall.at[me], qall)
    for j in range(n):
        queries[j * rows:(j + 1) * rows] = qall[j]
    each(n // 2, lambda k: core_step(0, k))
    loop(line, lambda k: line_step(1, k))

    per_block = max(1, min(heads, 256 // lats))
    lane = lax.broadcasted_iota(jnp.int32, (lats, LANES), 1)
    stat_max = jnp.zeros((lats, LANES), jnp.float32)
    stat_sum = jnp.zeros((lats, LANES), jnp.float32)
    for first in range(0, heads, per_block):
        folded = []
        for head in range(first, first + per_block):
            start, width = window(head, breadth)
            part_q = queries[:, start:start + width]
            part_q = jnp.where(head_mask(head, breadth, part_q.shape), part_q, 0.0)
            both = jnp.concatenate(halves(part_q), axis=0)
            look = gathered[0, :, :, start:start + width].astype(jnp.bfloat16)
            look = look.reshape(n * shard, width)
            raw = lax.dot_general(both, look, NT, preferred_element_type=jnp.float32)
            folded.append(raw[:lats] + raw[lats:])
        high, low = halves(jnp.concatenate(folded, axis=0))
        scores = lax.dot_general(high, source[...], NT, preferred_element_type=jnp.float32)
        scores += lax.dot_general(low, source[...], NT, preferred_element_type=jnp.float32)
        column = lax.broadcasted_iota(jnp.int32, scores.shape, 1)
        live = (column >= tok_count) & (column < tok_count + rows)
        for i in range(steps):
            live |= (column >= i * packed) & (column < i * packed + real)
        scores = jnp.where(live, scores, -jnp.inf)
        row_max = jnp.max(scores, axis=1, keepdims=True)
        terms = jnp.exp(scores - row_max).astype(jnp.bfloat16)
        row_sum = jnp.sum(terms.astype(jnp.float32), axis=1, keepdims=True)
        mixed = jnp.dot(terms, source[...], preferred_element_type=jnp.float32)
        high, low = halves(mixed)
        u_high[first * lats:(first + per_block) * lats] = high
        u_low[first * lats:(first + per_block) * lats] = low
        for i in range(per_block):
            stat_max = jnp.where(lane == first + i, row_max[i * lats:(i + 1) * lats], stat_max)
            stat_sum = jnp.where(lane == first + i, row_sum[i * lats:(i + 1) * lats], stat_sum)
        if first == 0:
            each(line, lambda k: far_step(1, k))
    each(n // 2, lambda k: core_step(1, k))

    wsum[...] = jnp.zeros_like(wsum)
    for head in range(heads):
        start, width = window(head, breadth)
        both = jnp.concatenate(
            [u_high[head * lats:(head + 1) * lats], u_low[head * lats:(head + 1) * lats]], axis=0
        )
        content = gathered[1, :, :, start:start + width].astype(jnp.bfloat16)
        raw = jnp.dot(both, content.reshape(n * shard, width), preferred_element_type=jnp.float32)
        raw = raw[:lats] + raw[lats:]
        wsum[:, start:start + width] += jnp.where(head_mask(head, breadth, raw.shape), raw, 0.0)
    for j in range(n):
        cut = slice(j * rows, (j + 1) * rows)
        part[j, :, :channels] = wsum[cut]
        part[j, :, channels:channels + LANES] = stat_max[cut]
        part[j, :, channels + LANES:] = stat_sum[cut]
    received[me] = part[me]
    swap_start(2, lambda j: part.at[j], received)
    swap_wait(2, lambda j: part.at[j], received)

    maxima = received[:, :, channels:channels + LANES]
    factor = jnp.exp(maxima - jnp.max(maxima, axis=0, keepdims=True))
    joint = jnp.sum(received[:, :, channels + LANES:] * factor, axis=0, keepdims=True)
    factor = factor / jnp.where(joint > 0.0, joint, 1.0)
    att_all[me] = jnp.zeros((rows, channels), jnp.float32)
    for head in range(heads):
        start, width = window(head, breadth)
        scaled = received[:, :, start:start + width] * factor[:, :, head:head + 1]
        scaled = jnp.sum(scaled, axis=0)
        keep = head_mask(head, breadth, scaled.shape)
        att_all[me, :, start:start + width] += jnp.where(keep, scaled, 0.0)
    swap_start(3, lambda j: att_all.at[me], att_all)
    swap_wait(3, lambda j: att_all.at[me], att_all)
    for j in range(n):
        wsum[j * rows:(j + 1) * rows] = att_all[j]
    att_low[...] = wsum[...].astype(jnp.bfloat16)
    cols_all[me] = jnp.dot(att_low[...], wo_ref[...], preferred_element_type=jnp.float32)
    swap_start(4, lambda j: cols_all.at[me], cols_all)
    swap_wait(4, lambda j: cols_all.at[me], cols_all)
    wide = wo_ref.shape[1]
    for j in range(n):
        attended_ref[:, j * wide:(j + 1) * wide] = cols_all[j]
    new_ref[...] = (probes_ref[...].astype(jnp.float32) + attended_ref[...]).astype(jnp.bfloat16)
    finish_sends(0)
    finish_sends(1)


def per_device(
    n,
    picture_feature_maps,
    partitioned_filter_tensor,
    picture_token_layer_scaling,
    summary_probes,
    summary_probe_layer_scaling,
    asking_projection_tensor,
    lookup_projection_tensor,
    content_projection_tensor,
    final_projection_tensor,
    sharpness_coefficient,
):
    channels = picture_feature_maps.shape[3]
    heads = sharpness_coefficient.shape[0]
    breadth = channels // heads
    lats = summary_probes.shape[0]
    frames, high_side, wide_side, _ = picture_feature_maps.shape
    at_once = 2 if frames % 2 == 0 else 1
    pitch = -(-(wide_side + 1) // 16) * 16
    flat = high_side * pitch
    real = at_once * high_side * wide_side
    packed = -(-real // 16) * 16
    pick = np.zeros((packed, at_once * flat), np.float32)
    for r in range(real):
        pick[r, r // wide_side * pitch + r % wide_side] = 1.0
    filters = partitioned_filter_tensor.reshape(-1, channels)
    tok_count = frames // at_once * packed
    lat_norm = layer_norm(summary_probes.astype(jnp.float32), summary_probe_layer_scaling).astype(
        jnp.bfloat16
    )
    shard = asking_projection_tensor.shape[0]
    rows = lats // n
    me = lax.axis_index("wide")
    lat_slice = lax.dynamic_slice_in_dim(lat_norm, me * shard, shard, 1)
    lat_own = lax.dynamic_slice_in_dim(lat_norm, me * rows, rows, 0)
    extra = -(-rows // 16) * 16
    lat_own = jnp.pad(lat_own, ((0, extra - rows), (0, 0)))
    sharp = jnp.repeat(sharpness_coefficient / math.sqrt(breadth), breadth)[None, :]
    lookup, content = lookup_projection_tensor, content_projection_tensor
    wire = jnp.bfloat16 if shard % 16 == 0 else jnp.float32
    lookup, content = lookup.astype(wire), content.astype(wire)
    vmem = pl.BlockSpec(memory_space=pltpu.VMEM)
    f32, bf16 = jnp.float32, jnp.bfloat16
    width = final_projection_tensor.shape[1]
    line = n // 4
    return pl.pallas_call(
        functools.partial(mixer, n, heads),
        out_shape=(
            jax.ShapeDtypeStruct((lats, channels), f32),
            jax.ShapeDtypeStruct((lats, channels), bf16),
        ),
        in_specs=[vmem] * 12,
        out_specs=(vmem, vmem),
        scratch_shapes=[
            pltpu.VMEM((2, n, shard, channels), wire),
            pltpu.VMEM((n, rows, channels), f32),
            pltpu.VMEM((n, rows, channels), f32),
            pltpu.VMEM((n, rows, channels), f32),
            pltpu.VMEM((lats, channels), f32),
            pltpu.VMEM((tok_count + extra, channels), bf16),
            pltpu.VMEM((heads * lats, channels), bf16),
            pltpu.VMEM((heads * lats, channels), bf16),
            pltpu.VMEM((lats, channels), f32),
            pltpu.VMEM((n, rows, channels + 2 * LANES), f32),
            pltpu.VMEM((n, rows, channels + 2 * LANES), f32),
            pltpu.VMEM((n, rows, channels), f32),
            pltpu.VMEM((lats, channels), bf16),
            pltpu.VMEM((n, lats, width), f32),
            pltpu.VMEM((at_once, high_side, pitch, channels), f32),
            pltpu.VMEM((at_once, 3, flat + 2 * pitch, channels), bf16),
            pltpu.VMEM((at_once * flat, channels), f32),
            pltpu.SemaphoreType.DMA((2, line)),
            pltpu.SemaphoreType.DMA((2, line)),
            pltpu.SemaphoreType.DMA((2, 2 * line)),
            pltpu.SemaphoreType.DMA((2, n)),
            pltpu.SemaphoreType.DMA((5, n)),
            pltpu.SemaphoreType.DMA((5, n)),
        ],
        compiler_params=pltpu.CompilerParams(
            collective_id=0, has_side_effects=True, vmem_limit_bytes=56 * 1024 * 1024
        ),
    )(
        picture_feature_maps, filters, picture_token_layer_scaling[None, :],
        jnp.asarray(pick, bf16), lat_own, lat_slice, summary_probes, sharp,
        asking_projection_tensor, lookup, content, final_projection_tensor,
    )


def solution(mesh):
    placed = (
        P(("groups", "wide"), None, None, None),
        P(),
        P(),
        P(),
        P(),
        P("wide", None),
        P("wide", None),
        P("wide", None),
        P(None, "wide"),
        P(),
    )
    return jax.shard_map(
        functools.partial(per_device, mesh.shape["wide"]),
        mesh=mesh,
        in_specs=placed,
        out_specs=(P("groups", None), P("groups", None)),
        check_vma=False,
    )
```

```python
import functools
import math

import jax
import jax.numpy as jnp
import numpy as np
from jax import lax
from jax.experimental import pallas as pl
from jax.experimental.pallas import tpu as pltpu
from jax.sharding import PartitionSpec as P

RESIDUAL_SCALE = 0.2
EPSILON = 1e-06
LANES = 128
NT = (((1,), (1,)), ((), ()))


def layer_norm(values, gain):
    center = values - jnp.mean(values, axis=-1, keepdims=True)
    spread = jnp.mean(center * center, axis=-1, keepdims=True)
    return center * lax.rsqrt(spread + EPSILON) * gain


def window(head, breadth):
    start = head * breadth // LANES * LANES
    stop = -(-(head + 1) * breadth // LANES) * LANES
    return start, stop - start


def head_mask(head, breadth, shape):
    start, width = window(head, breadth)
    lane = lax.broadcasted_iota(jnp.int32, shape, len(shape) - 1) + start
    return (lane >= head * breadth) & (lane < (head + 1) * breadth)


def halves(values):
    high = values.astype(jnp.bfloat16)
    low = (values - high.astype(jnp.float32)).astype(jnp.bfloat16)
    return high, low


def mixer(
    n, heads,
    maps_ref, filter_ref, gain_ref, pick_ref, lat_own_ref, lat_slice_ref, probes_ref, sharp_ref,
    wq_ref, wk_ref, wv_ref, wo_ref,
    attended_ref, new_ref,
    gathered, qpart, qrecv, qall, queries, source, u_high, u_low,
    wsum, part, received, att_all, att_low, cols_all,
    plain, act, summed,
    z_send, y_send, x_send, core_send, side_send, w_recv, side_recv, swap_send, swap_recv,
):
    channels = sharp_ref.shape[1]
    breadth = channels // heads
    lats = probes_ref.shape[0]
    rows = lats // n
    shard = wk_ref.shape[0]
    line = n // 4
    me = lax.axis_index("wide")
    core = lax.rem(me, 2)
    side = lax.rem(me // 2, 2)
    at = me // 4
    team = lax.axis_index("groups")
    odd = lax.rem(team, 2)
    third = shard // 3
    piece = pl.ds(pl.multiple_of(odd * third, third), 2 * third)
    spare = pl.ds(pl.multiple_of(odd * 2 * third, third), third)
    lacking = pl.ds(pl.multiple_of((1 - odd) * 2 * third, third), third)
    weights = (wk_ref, wv_ref)

    def place(a, b, c):
        return a * 4 + b * 2 + c

    def remote(src, dst, send, recv, target):
        return pltpu.make_async_remote_copy(
            src_ref=src, dst_ref=dst, send_sem=send, recv_sem=recv,
            device_id={"wide": target}, device_id_type=pl.DeviceIdType.MESH,
        )

    def ring(k):
        return lax.rem(me + k, n)

    def back(k):
        return lax.rem(me + n - k, n)

    def loop(count, body):
        def step(k, carry):
            body(k)
            return carry
        lax.fori_loop(1, count, step, 0)

    def swap(slot, src_of, dst, target, owner):
        return remote(
            src_of(target), dst.at[owner], swap_send.at[slot, target], swap_recv.at[slot, owner], target
        )

    def swap_start(slot, src_of, dst):
        loop(n, lambda k: swap(slot, src_of, dst, ring(k), me).start())

    def swap_wait(slot, src_of, dst):
        loop(n, lambda k: swap(slot, src_of, dst, ring(k), me).wait_send())
        loop(n, lambda k: swap(slot, src_of, dst, me, back(k)).wait_recv())

    def along(w, k):
        return remote(
            weights[w].at[piece], gathered.at[w, me, piece], z_send.at[w, k], w_recv.at[w, me],
            place(lax.rem(at + k, line), side, core),
        )

    def across(w, a):
        slab = gathered.at[w, place(a, side, core), piece]
        return remote(
            slab, slab, y_send.at[w, a], w_recv.at[w, place(a, side, core)],
            place(at, 1 - side, core),
        )

    def beside(w, a, b, rows_of):
        slab = gathered.at[w, place(a, b, core), rows_of]
        return pltpu.make_async_remote_copy(
            src_ref=slab, dst_ref=slab, send_sem=x_send.at[w, a * 2 + b],
            recv_sem=side_recv.at[w, place(a, b, core)],
            device_id={"groups": team + 1 - 2 * odd, "wide": me},
            device_id_type=pl.DeviceIdType.MESH,
        )

    def over(w, a, b):
        slab = gathered.at[w, place(a, b, core), piece]
        return remote(
            slab, slab, core_send.at[w, a * 2 + b], w_recv.at[w, place(a, b, core)],
            place(at, side, 1 - core),
        )

    def over_side(w, a, b):
        slab = gathered.at[w, place(a, b, core), lacking]
        return remote(
            slab, slab, side_send.at[w, a * 2 + b], side_recv.at[w, place(a, b, core)],
            place(at, side, 1 - core),
        )

    def arrival(w, owner, rows_of, sems):
        slab = gathered.at[w, owner, rows_of]
        remote(
            slab, slab, z_send.at[w, 0], sems.at[w, owner], place(at, side, 1 - core)
        ).wait_recv()

    def line_step(w, k):
        a = lax.rem(at + line - k, line)
        arrival(w, place(a, side, core), piece, w_recv)
        across(w, a).start()
        beside(w, a, side, spare).start()
        over(w, a, side).start()

    def far_step(w, k):
        a = lax.rem(at + line - k, line)
        arrival(w, place(a, 1 - side, core), piece, w_recv)
        beside(w, a, 1 - side, spare).start()
        over(w, a, 1 - side).start()

    def side_step(w, k):
        a = lax.rem(at + line - k, line)

        @pl.when(k > 0)
        def _():
            arrival(w, place(a, side, core), lacking, side_recv)
            over_side(w, a, side).start()

        arrival(w, place(a, 1 - side, core), lacking, side_recv)
        over_side(w, a, 1 - side).start()

    def core_step(w, k):
        owner = place(k // 2, lax.rem(k, 2), 1 - core)
        arrival(w, owner, piece, w_recv)
        arrival(w, owner, lacking, side_recv)

    def finish_sends(w):
        def one(k, carry):
            a = lax.rem(at + line - k, line)
            across(w, a).wait_send()
            over(w, a, 0).wait_send()
            over(w, a, 1).wait_send()
            over_side(w, a, 0).wait_send()
            over_side(w, a, 1).wait_send()
            beside(w, a, 1 - side, spare).wait_send()

            @pl.when(k > 0)
            def _():
                beside(w, a, side, spare).wait_send()
            return carry
        loop(line, lambda k: along(w, k).wait_send())
        lax.fori_loop(0, line, one, 0)

    def each(count, body):
        def step(k, carry):
            body(k)
            return carry
        lax.fori_loop(0, count, step, 0)

    barrier = pltpu.get_barrier_semaphore()
    loop(n, lambda k: pl.semaphore_signal(
        barrier, inc=1, device_id={"wide": ring(k)}, device_id_type=pl.DeviceIdType.MESH))
    pl.semaphore_signal(
        barrier, inc=1, device_id={"groups": team + 1 - 2 * odd, "wide": me},
        device_id_type=pl.DeviceIdType.MESH)
    pl.semaphore_wait(barrier, n)

    partial = jnp.dot(lat_slice_ref[...], wq_ref[...], preferred_element_type=jnp.float32)
    for j in range(n):
        qpart[j] = partial[j * rows:(j + 1) * rows]
    qrecv[me] = qpart[me]
    swap_start(0, lambda j: qpart.at[j], qrecv)

    def send_own(w):
        gathered[w, me] = weights[w][...]
        loop(line, lambda k: along(w, k).start())
        across(w, at).start()
        over(w, at, side).start()
        over_side(w, at, side).start()

    send_own(0)
    frames, high_side, wide_side = maps_ref.shape[:3]
    group = filter_ref.shape[0] // 9
    at_once = plain.shape[0]
    pitch = plain.shape[2]
    flat = high_side * pitch
    steps = frames // at_once
    packed = pick_ref.shape[0]
    real = at_once * high_side * wide_side
    tok_count = steps * packed
    plain[...] = jnp.zeros_like(plain)
    act[...] = jnp.zeros_like(act)
    source[tok_count:] = lat_own_ref[...]

    def convolve(i):
        for f in range(at_once):
            plain[f, :, :wide_side] = maps_ref[i * at_once + f].astype(jnp.float32)
            g = jax.nn.gelu(plain[f]).reshape(flat, channels)
            act[f, 0, pitch:pitch + flat] = pltpu.roll(g, 1, 0).astype(jnp.bfloat16)
            act[f, 1, pitch:pitch + flat] = g.astype(jnp.bfloat16)
            act[f, 2, pitch:pitch + flat] = pltpu.roll(g, flat - 1, 0).astype(jnp.bfloat16)
        for c in range(channels // group):
            cut = slice(c * group, (c + 1) * group)
            taps = jnp.concatenate([
                jnp.concatenate([
                    act[f, dx, dy * pitch:dy * pitch + flat, cut]
                    for dy in range(3) for dx in range(3)
                ], axis=1)
                for f in range(at_once)
            ], axis=0)
            summed[:, cut] = jnp.dot(
                taps, filter_ref[:, cut], preferred_element_type=jnp.float32)
        normed = []
        for f in range(at_once):
            rows_of = slice(f * flat, (f + 1) * flat)
            value = plain[f].reshape(flat, channels) + RESIDUAL_SCALE * summed[rows_of]
            normed.append(layer_norm(value, gain_ref[...]).astype(jnp.bfloat16))
        dense = jnp.dot(
            pick_ref[...], jnp.concatenate(normed, axis=0), preferred_element_type=jnp.float32)
        where = pl.multiple_of(i * packed, 16)
        source[pl.ds(where, packed)] = dense.astype(jnp.bfloat16)

    def conv_and_pass(i, carry):
        convolve(i)

        @pl.when((i >= 1) & (i < line))
        def _():
            line_step(0, i)
        return carry

    lax.fori_loop(0, steps, conv_and_pass, 0)

    def pass_on(k, carry):
        line_step(0, k)
        return carry

    lax.fori_loop(min(steps, line), line, pass_on, 0)
    send_own(1)

    swap_wait(0, lambda j: qpart.at[j], qrecv)
    qall[me] = jnp.sum(qrecv[...], axis=0) * sharp_ref[...]
    swap_start(1, lambda j: qall.at[me], qall)

    each(line, lambda k: far_step(0, k))
    each(line, lambda k: side_step(0, k))
    swap_wait(1, lambda j: qall.at[me], qall)
    for j in range(n):
        queries[j * rows:(j + 1) * rows] = qall[j]
    each(n // 2, lambda k: core_step(0, k))
    loop(line, lambda k: line_step(1, k))

    per_block = max(1, min(heads, 256 // lats))
    lane = lax.broadcasted_iota(jnp.int32, (lats, LANES), 1)
    stat_max = jnp.zeros((lats, LANES), jnp.float32)
    stat_sum = jnp.zeros((lats, LANES), jnp.float32)
    for first in range(0, heads, per_block):
        folded = []
        for head in range(first, first + per_block):
            start, width = window(head, breadth)
            part_q = queries[:, start:start + width]
            part_q = jnp.where(head_mask(head, breadth, part_q.shape), part_q, 0.0)
            both = jnp.concatenate(halves(part_q), axis=0)
            look = gathered[0, :, :, start:start + width].astype(jnp.bfloat16)
            look = look.reshape(n * shard, width)
            raw = lax.dot_general(both, look, NT, preferred_element_type=jnp.float32)
            folded.append(raw[:lats] + raw[lats:])
        high, low = halves(jnp.concatenate(folded, axis=0))
        scores = lax.dot_general(high, source[...], NT, preferred_element_type=jnp.float32)
        scores += lax.dot_general(low, source[...], NT, preferred_element_type=jnp.float32)
        column = lax.broadcasted_iota(jnp.int32, scores.shape, 1)
        live = (column >= tok_count) & (column < tok_count + rows)
        for i in range(steps):
            live |= (column >= i * packed) & (column < i * packed + real)
        scores = jnp.where(live, scores, -jnp.inf)
        row_max = jnp.max(scores, axis=1, keepdims=True)
        terms = jnp.exp(scores - row_max).astype(jnp.bfloat16)
        row_sum = jnp.sum(terms.astype(jnp.float32), axis=1, keepdims=True)
        mixed = jnp.dot(terms, source[...], preferred_element_type=jnp.float32)
        high, low = halves(mixed)
        u_high[first * lats:(first + per_block) * lats] = high
        u_low[first * lats:(first + per_block) * lats] = low
        for i in range(per_block):
            stat_max = jnp.where(lane == first + i, row_max[i * lats:(i + 1) * lats], stat_max)
            stat_sum = jnp.where(lane == first + i, row_sum[i * lats:(i + 1) * lats], stat_sum)
        if first == 0:
            each(line, lambda k: far_step(1, k))
        if first == per_block:
            each(line, lambda k: side_step(1, k))
    each(n // 2, lambda k: core_step(1, k))

    wsum[...] = jnp.zeros_like(wsum)
    for head in range(heads):
        start, width = window(head, breadth)
        both = jnp.concatenate(
            [u_high[head * lats:(head + 1) * lats], u_low[head * lats:(head + 1) * lats]], axis=0
        )
        content = gathered[1, :, :, start:start + width].astype(jnp.bfloat16)
        raw = jnp.dot(both, content.reshape(n * shard, width), preferred_element_type=jnp.float32)
        raw = raw[:lats] + raw[lats:]
        wsum[:, start:start + width] += jnp.where(head_mask(head, breadth, raw.shape), raw, 0.0)
    for j in range(n):
        cut = slice(j * rows, (j + 1) * rows)
        part[j, :, :channels] = wsum[cut]
        part[j, :, channels:channels + LANES] = stat_max[cut]
        part[j, :, channels + LANES:] = stat_sum[cut]
    received[me] = part[me]
    swap_start(2, lambda j: part.at[j], received)
    swap_wait(2, lambda j: part.at[j], received)

    maxima = received[:, :, channels:channels + LANES]
    factor = jnp.exp(maxima - jnp.max(maxima, axis=0, keepdims=True))
    joint = jnp.sum(received[:, :, channels + LANES:] * factor, axis=0, keepdims=True)
    factor = factor / jnp.where(joint > 0.0, joint, 1.0)
    att_all[me] = jnp.zeros((rows, channels), jnp.float32)
    for head in range(heads):
        start, width = window(head, breadth)
        scaled = received[:, :, start:start + width] * factor[:, :, head:head + 1]
        scaled = jnp.sum(scaled, axis=0)
        keep = head_mask(head, breadth, scaled.shape)
        att_all[me, :, start:start + width] += jnp.where(keep, scaled, 0.0)
    swap_start(3, lambda j: att_all.at[me], att_all)
    swap_wait(3, lambda j: att_all.at[me], att_all)
    for j in range(n):
        wsum[j * rows:(j + 1) * rows] = att_all[j]
    att_low[...] = wsum[...].astype(jnp.bfloat16)
    cols = jnp.dot(att_low[...], wo_ref[...], preferred_element_type=jnp.float32)
    cols_all[me] = cols.astype(jnp.bfloat16)
    swap_start(4, lambda j: cols_all.at[me], cols_all)
    swap_wait(4, lambda j: cols_all.at[me], cols_all)
    wide = wo_ref.shape[1]
    for j in range(n):
        attended_ref[:, j * wide:(j + 1) * wide] = cols_all[j].astype(jnp.float32)
    new_ref[...] = (probes_ref[...].astype(jnp.float32) + attended_ref[...]).astype(jnp.bfloat16)
    finish_sends(0)
    finish_sends(1)


def per_device(
    n,
    picture_feature_maps,
    partitioned_filter_tensor,
    picture_token_layer_scaling,
    summary_probes,
    summary_probe_layer_scaling,
    asking_projection_tensor,
    lookup_projection_tensor,
    content_projection_tensor,
    final_projection_tensor,
    sharpness_coefficient,
):
    channels = picture_feature_maps.shape[3]
    heads = sharpness_coefficient.shape[0]
    breadth = channels // heads
    lats = summary_probes.shape[0]
    frames, high_side, wide_side, _ = picture_feature_maps.shape
    at_once = 2 if frames % 2 == 0 else 1
    pitch = -(-(wide_side + 1) // 16) * 16
    flat = high_side * pitch
    real = at_once * high_side * wide_side
    packed = -(-real // 16) * 16
    pick = np.zeros((packed, at_once * flat), np.float32)
    for r in range(real):
        pick[r, r // wide_side * pitch + r % wide_side] = 1.0
    filters = partitioned_filter_tensor.reshape(-1, channels)
    tok_count = frames // at_once * packed
    lat_norm = layer_norm(summary_probes.astype(jnp.float32), summary_probe_layer_scaling).astype(
        jnp.bfloat16
    )
    shard = asking_projection_tensor.shape[0]
    rows = lats // n
    me = lax.axis_index("wide")
    lat_slice = lax.dynamic_slice_in_dim(lat_norm, me * shard, shard, 1)
    lat_own = lax.dynamic_slice_in_dim(lat_norm, me * rows, rows, 0)
    extra = -(-rows // 16) * 16
    lat_own = jnp.pad(lat_own, ((0, extra - rows), (0, 0)))
    sharp = jnp.repeat(sharpness_coefficient / math.sqrt(breadth), breadth)[None, :]
    lookup, content = lookup_projection_tensor, content_projection_tensor
    wire = jnp.bfloat16 if shard % 16 == 0 else jnp.float32
    lookup, content = lookup.astype(wire), content.astype(wire)
    vmem = pl.BlockSpec(memory_space=pltpu.VMEM)
    f32, bf16 = jnp.float32, jnp.bfloat16
    width = final_projection_tensor.shape[1]
    line = n // 4
    return pl.pallas_call(
        functools.partial(mixer, n, heads),
        out_shape=(
            jax.ShapeDtypeStruct((lats, channels), f32),
            jax.ShapeDtypeStruct((lats, channels), bf16),
        ),
        in_specs=[vmem] * 12,
        out_specs=(vmem, vmem),
        scratch_shapes=[
            pltpu.VMEM((2, n, shard, channels), wire),
            pltpu.VMEM((n, rows, channels), f32),
            pltpu.VMEM((n, rows, channels), f32),
            pltpu.VMEM((n, rows, channels), f32),
            pltpu.VMEM((lats, channels), f32),
            pltpu.VMEM((tok_count + extra, channels), bf16),
            pltpu.VMEM((heads * lats, channels), bf16),
            pltpu.VMEM((heads * lats, channels), bf16),
            pltpu.VMEM((lats, channels), f32),
            pltpu.VMEM((n, rows, channels + 2 * LANES), f32),
            pltpu.VMEM((n, rows, channels + 2 * LANES), f32),
            pltpu.VMEM((n, rows, channels), f32),
            pltpu.VMEM((lats, channels), bf16),
            pltpu.VMEM((n, lats, width), bf16),
            pltpu.VMEM((at_once, high_side, pitch, channels), f32),
            pltpu.VMEM((at_once, 3, flat + 2 * pitch, channels), bf16),
            pltpu.VMEM((at_once * flat, channels), f32),
            pltpu.SemaphoreType.DMA((2, line)),
            pltpu.SemaphoreType.DMA((2, line)),
            pltpu.SemaphoreType.DMA((2, 2 * line)),
            pltpu.SemaphoreType.DMA((2, 2 * line)),
            pltpu.SemaphoreType.DMA((2, 2 * line)),
            pltpu.SemaphoreType.DMA((2, n)),
            pltpu.SemaphoreType.DMA((2, n)),
            pltpu.SemaphoreType.DMA((5, n)),
            pltpu.SemaphoreType.DMA((5, n)),
        ],
        compiler_params=pltpu.CompilerParams(
            collective_id=0, has_side_effects=True, vmem_limit_bytes=56 * 1024 * 1024
        ),
    )(
        picture_feature_maps, filters, picture_token_layer_scaling[None, :],
        jnp.asarray(pick, bf16), lat_own, lat_slice, summary_probes, sharp,
        asking_projection_tensor, lookup, content, final_projection_tensor,
    )


def solution(mesh):
    placed = (
        P(("groups", "wide"), None, None, None),
        P(),
        P(),
        P(),
        P(),
        P("wide", None),
        P("wide", None),
        P("wide", None),
        P(None, "wide"),
        P(),
    )
    return jax.shard_map(
        functools.partial(per_device, mesh.shape["wide"]),
        mesh=mesh,
        in_specs=placed,
        out_specs=(P("groups", None), P("groups", None)),
        check_vma=False,
    )
```
